32 devices in a mesh: groups: 2 (over y), dp: 4 (over z), query: 2 (over x), mp: 2 (over core).
Axes of the slice: x: 2, y: 2, z: 4, core: 2. Of those that a mesh axis runs over, the one named last changes fastest.
Arguments:
- hidden_in: bfloat16 [16, 192, 14336], P(('groups', 'dp'), 'query', 'mp'), parts along dimension 0, may hold values from -6 to 6
- out_grad: bfloat16 [16, 192, 4096], P(('groups', 'dp'), 'query', 'mp'), parts along dimension 0, may hold values from -6 to 6
- proj_in: bfloat16 [32, 14336], P(None, 'mp'), may hold values from -0.046875 to 0.046875
- proj_out: bfloat16 [32, 4096], P(None, 'mp'), may hold values from -0.09375 to 0.09375
- lengths: int32 [16], P(('groups', 'dp')), parts along dimension 0, may hold values from 48 to 192
- query_grads: float32 [512, 1024], P(('groups', 'query', 'dp')), parts along dimension 0, may hold values from -4 to 4
Outputs:
- scores: float32 [16, 256], P(('groups', 'dp'), 'query'), parts along dimension 0
The draws below stay inside these ranges and needn't reach their ends.
There are 2 independent parts, one for each index of `groups`. The reference program is written for one: setup_inputs(seed, part) draws one part's arguments, and reference() takes and returns one part's arrays. A program takes and returns all parts, laid end to end along the dimension named above; an argument that names none is the same for every part. Nothing has to cross between parts.
All inputs are finite; a program needn't handle non-finite values.
Results may differ from the reference program's by a relative error of at most 0.00035.
Values sent between devices are 32-bit elements; how exact they have to be, the bound alone decides.
A program may use at most 64 MiB of HBM per device.

```python
import jax
import jax.numpy as jnp
from jax import lax

D = 4096
FF = 14336
RANK = 32
EXAMPLES = 8
SEQ = 192
QUERIES = 256


def plant(array, key, smallest, largest):
    longest = array.shape.index(max(array.shape))
    spots = []
    for shift in (0, 1):
        where = [jax.random.randint(jax.random.fold_in(key, axis), (), 0, length) for axis, length in enumerate(array.shape)]
        where[longest] = (where[longest] + shift) % array.shape[longest]
        spots.append(tuple(where))
    return array.at[spots[0]].set(smallest).at[spots[1]].set(largest)


def steps_of(own_key, shape, pieces, low, high):
    def one(dim, parts):
        draws = jax.random.uniform(jax.random.fold_in(jax.random.fold_in(own_key, 6), dim), (parts,), jnp.float32, low / len(pieces), high / len(pieces))
        return jnp.repeat(jnp.exp(draws), shape[dim] // parts).reshape((-1,) + (1,) * (len(shape) - dim - 1))

    loudness = one(*pieces[0])
    for cut in pieces[1:]:
        loudness = loudness * one(*cut)
    return loudness


def centred(rng, extent, deviation, reach, cuts=(), kind=jnp.bfloat16):
    gain = steps_of(rng, extent, cuts, -0.22, 0.18) if cuts else 1.0
    array = jax.random.normal(rng, extent, jnp.float32) * deviation * gain
    return jnp.minimum(jnp.maximum(array, -reach), reach).astype(kind)


def setup_inputs(seed: int = 0, part: int = 0) -> dict:
    streams_of = jax.random.split(jax.random.key(seed), 7)
    own_keys = jax.random.split(jax.random.fold_in(streams_of[6], part), 7)
    return {
        "hidden_in": centred(own_keys[0], (EXAMPLES, SEQ, FF), 1.0, 6.0, ((0, 4), (1, 2), (2, 2))),
        "out_grad": centred(own_keys[1], (EXAMPLES, SEQ, D), 1.0, 6.0, ((0, 4), (1, 2), (2, 2))),
        "proj_in": centred(streams_of[2], (RANK, FF), FF ** -0.5, 0.046875, ((1, 2),)),
        "proj_out": centred(streams_of[3], (RANK, D), D ** -0.5, 0.09375, ((1, 2),)),
        "lengths": plant(jax.random.randint(own_keys[4], (EXAMPLES,), max(1, SEQ // 4), SEQ + 1), jax.random.fold_in(own_keys[4], 1), max(1, SEQ // 4), SEQ).astype(jnp.int32),
        "query_grads": centred(own_keys[5], (QUERIES, RANK * RANK), 0.25, 4.0, ((0, 8),), jnp.float32),
    }


DAMPING = 1.0

def reference(hidden_in, out_grad, proj_in, proj_out, lengths, query_grads):
    positions = jnp.arange(SEQ)

    def one_example(inputs):
        hidden_rows, grad_rows, used = inputs
        in_proj = jnp.dot(hidden_rows.astype(jnp.float32), proj_in.T.astype(jnp.float32), preferred_element_type=jnp.float32)
        out_proj = jnp.dot(grad_rows.astype(jnp.float32), proj_out.T.astype(jnp.float32), preferred_element_type=jnp.float32)
        weights = jnp.where(positions < used, 1.0, 0.0).astype(jnp.float32) / jnp.sqrt(used.astype(jnp.float32))
        grads = jnp.dot((out_proj * weights[:, None]).T, in_proj, precision=lax.Precision.HIGHEST)
        return grads.reshape(-1)
    vectors = lax.map(one_example, (hidden_in, out_grad, lengths))
    fisher = jnp.dot(vectors.T, vectors, precision=lax.Precision.HIGHEST) / EXAMPLES
    damped = fisher + DAMPING * jnp.eye(RANK * RANK, dtype=jnp.float32)
    solved = jnp.linalg.solve(damped, query_grads.T)
    return jnp.dot(vectors, solved, precision=lax.Precision.HIGHEST)
```

```python
import functools

import jax
import jax.numpy as jnp
from jax import lax
from jax.experimental import pallas as pl
from jax.experimental.pallas import tpu as pltpu
from jax.sharding import PartitionSpec as P

DAMPING = 1.0
LANES = 128
SUBLANES = 8
MESH = pl.DeviceIdType.MESH
LAST = (((1,), (1,)), ((), ()))


def dot_last(left, right, precision=None):
    return lax.dot_general(
        left, right, LAST, precision=precision, preferred_element_type=jnp.float32
    )


def each(count, body):
    if count <= 16:
        for step in range(1, count):
            body(step)
    else:
        lax.fori_loop(1, count, lambda step, carry: (body(step), carry)[1], 0)


def solve_few(vectors, rhs, shift):
    total, width = rhs.shape
    rows = lax.broadcasted_iota(jnp.int32, (total, width), 0)
    columns = []
    for j in range(total):
        column = jnp.sum(vectors * vectors[j : j + 1], axis=1, keepdims=True)
        column = jnp.broadcast_to(column, (total, width))
        columns.append(jnp.where(rows == j, column + shift, column))
    for k in range(total):
        pivot = columns[k]
        inverse = 1.0 / pivot[k : k + 1]

        def step(array):
            own = array[k : k + 1] * inverse
            return jnp.where(rows == k, own, array - pivot * own)

        rhs = step(rhs)
        columns = [step(c) if j > k else c for j, c in enumerate(columns)]
    return rhs


def solve_many(vectors, rhs, shift):
    total, width = rhs.shape
    gram = dot_last(vectors, vectors, lax.Precision.HIGHEST)
    rows = lax.broadcasted_iota(jnp.int32, (total, total), 0)
    columns = lax.broadcasted_iota(jnp.int32, (total, total), 1)
    rhs_rows = lax.broadcasted_iota(jnp.int32, (total, width), 0)
    gram = jnp.where(rows == columns, gram + shift, gram)

    def step(k, carry):
        gram, rhs = carry
        column = jnp.sum(jnp.where(columns == k, gram, 0.0), axis=1, keepdims=True)
        row = jnp.sum(jnp.where(rows == k, gram, 0.0), axis=0, keepdims=True)
        rhs_row = jnp.sum(jnp.where(rhs_rows == k, rhs, 0.0), axis=0, keepdims=True)
        pivot = jnp.sum(
            jnp.where(columns[:1] == k, row, 0.0), axis=1, keepdims=True
        )
        row, rhs_row = row / pivot, rhs_row / pivot
        gram = jnp.where(rows == k, row, gram - column * row)
        rhs = jnp.where(rhs_rows == k, rhs_row, rhs - column * rhs_row)
        return gram, rhs

    return lax.fori_loop(0, total, step, (gram, rhs))[1]


def kernel(
    sizes,
    chunks,
    hidden_hbm,
    grad_hbm,
    proj_in_hbm,
    proj_out_hbm,
    lengths_ref,
    query_hbm,
    out_ref,
    hidden,
    grad,
    proj_in,
    proj_out,
    query,
    sums,
    pair,
    grads,
    sent,
    landed,
    load_sem,
    hidden_sem,
    pair_send,
    pair_recv,
    grads_send,
    grads_recv,
    score_send,
    score_recv,
):
    dp_size, query_size, mp_size = sizes
    assert mp_size == 2
    my_dp, my_query, my_mp = (lax.axis_index(a) for a in ("dp", "query", "mp"))
    other = 1 - my_mp
    examples, seq, width = hidden.shape
    rank = proj_in.shape[0]
    queries = query.shape[0]
    planes = dp_size * query_size
    me = my_query * dp_size + my_dp
    total = dp_size * examples
    repeat = LANES // rank
    pieces = rank // repeat
    step_width = width // chunks

    def load(source, target, sem):
        copy = pltpu.make_async_copy(source, target, sem)
        copy.start()
        return copy

    proj_out_copy = load(proj_out_hbm, proj_out, load_sem.at[0])
    grad_copy = load(grad_hbm, grad, load_sem.at[1])
    hidden_copies = []
    for c in range(chunks):
        part = pl.ds(c * step_width, step_width)
        hidden_copies.append(
            (
                load(proj_in_hbm.at[:, part], proj_in.at[:, part], hidden_sem.at[0, c]),
                load(hidden_hbm.at[:, :, part], hidden.at[:, :, part], hidden_sem.at[1, c]),
            )
        )
    query_copy = load(query_hbm, query, load_sem.at[2])

    barrier = pltpu.get_barrier_semaphore()

    def place(step):
        slot = lax.rem(me + step, planes)
        return slot, {"dp": lax.rem(slot, dp_size), "query": slot // dp_size}

    def greet(step):
        pl.semaphore_signal(barrier, inc=1, device_id=place(step)[1], device_id_type=MESH)

    pl.semaphore_signal(barrier, inc=1, device_id={"mp": other}, device_id_type=MESH)
    each(planes, greet)

    proj_out_copy.wait()
    to_row = lax.broadcasted_iota(jnp.int32, (rank, rank), 0)
    from_row = lax.broadcasted_iota(jnp.int32, (rank, rank), 1)
    wanted = repeat * lax.rem(to_row, pieces) + to_row // pieces
    order = jnp.where(from_row == wanted, 1.0, 0.0).astype(jnp.bfloat16)
    ordered = jnp.dot(
        order, proj_out[...], preferred_element_type=jnp.float32
    ).astype(jnp.bfloat16)
    grad_copy.wait()
    for e in range(examples):
        sums[0, e] = dot_last(ordered, grad[e])

    pl.semaphore_wait(barrier, planes)

    def exchange(which):
        copy = pltpu.make_async_remote_copy(
            src_ref=sums.at[which],
            dst_ref=pair.at[which],
            send_sem=pair_send.at[which],
            recv_sem=pair_recv.at[which],
            device_id={"mp": other},
            device_id_type=MESH,
        )
        copy.start()
        return copy

    out_exchange = exchange(0)
    in_sums = [jnp.zeros((rank, seq), jnp.float32) for _ in range(examples)]
    for c in range(chunks):
        for copy in hidden_copies[c]:
            copy.wait()
        part = pl.ds(c * step_width, step_width)
        for e in range(examples):
            in_sums[e] += dot_last(proj_in[:, part], hidden[e, :, part])
    for e in range(examples):
        sums[1, e] = in_sums[e]
    in_exchange = exchange(1)
    query_copy.wait()
    out_exchange.wait()
    positions = my_query * seq + lax.broadcasted_iota(jnp.int32, (1, seq), 1)
    weighted = []
    for e in range(examples):
        used = jnp.full((1, seq), lengths_ref[e], jnp.int32)
        weights = jnp.where(positions < used, 1.0 / jnp.sqrt(used.astype(jnp.float32)), 0.0)
        weighted.append((sums[0, e] + pair[0, e]) * weights)
    in_exchange.wait()
    lanes = lax.broadcasted_iota(jnp.int32, (pieces, LANES), 1) // rank
    for e in range(examples):
        inputs = sums[1, e] + pair[1, e]
        product = dot_last(
            weighted[e], jnp.concatenate([inputs] * repeat, axis=0), lax.Precision.HIGHEST
        )
        flat = product[:pieces]
        for r in range(1, repeat):
            flat = jnp.where(lanes == r, product[r * pieces : (r + 1) * pieces], flat)
        grads[me, e * pieces : (e + 1) * pieces] = flat

    def grads_copy(slot, target):
        return pltpu.make_async_remote_copy(
            src_ref=grads.at[slot],
            dst_ref=grads.at[slot],
            send_sem=grads_send.at[target],
            recv_sem=grads_recv.at[slot],
            device_id=target_id(target),
            device_id_type=MESH,
        )

    def target_id(slot):
        return {"dp": lax.rem(slot, dp_size), "query": slot // dp_size}

    def send_grads(step):
        grads_copy(me, place(step)[0]).start()

    def wait_grads(step):
        slot = place(step)[0]
        grads_copy(slot, slot).wait_recv()

    def wait_sent(step):
        grads_copy(me, place(step)[0]).wait_send()

    each(planes, send_grads)
    each(planes, wait_grads)

    pieces_of = []
    flat_grads = grads.reshape(planes * examples * pieces, LANES)
    for p in range(pieces):
        piece = flat_grads[pl.ds(p, total, stride=pieces)]
        for q in range(1, query_size):
            piece += flat_grads[pl.ds(q * total * pieces + p, total, stride=pieces)]
        pieces_of.append(piece)
    vectors = jnp.concatenate(pieces_of, axis=1)
    blocks = LANES // queries
    rhs = dot_last(
        vectors, jnp.concatenate([query[...]] * blocks, axis=0), lax.Precision.HIGHEST
    )
    shift = DAMPING * total
    solve = solve_few if total <= SUBLANES else solve_many
    solved = solve(vectors, rhs * shift, shift)
    block_of_lane = lax.broadcasted_iota(jnp.int32, (total, LANES), 1) // queries
    solved = jnp.where(block_of_lane == lax.rem(my_dp, blocks), solved, 0.0)
    for d in range(dp_size):
        sent[d, :examples] = solved[d * examples : (d + 1) * examples]

    def score_copy(slot, target):
        return pltpu.make_async_remote_copy(
            src_ref=sent.at[target],
            dst_ref=landed.at[slot],
            send_sem=score_send.at[target],
            recv_sem=score_recv.at[slot],
            device_id={"dp": target},
            device_id_type=MESH,
        )

    def send_score(step):
        score_copy(my_dp, lax.rem(my_dp + step, dp_size)).start()

    def wait_score(step):
        slot = lax.rem(my_dp + step, dp_size)
        score_copy(slot, slot).wait_recv()

    def wait_score_sent(step):
        score_copy(my_dp, lax.rem(my_dp + step, dp_size)).wait_send()

    each(dp_size, send_score)
    landed[my_dp] = sent[my_dp]
    each(planes, wait_sent)
    each(dp_size, wait_score)
    for b in range(dp_size // blocks):
        block = landed[b * blocks]
        for d in range(b * blocks + 1, (b + 1) * blocks):
            block += landed[d]
        out_ref[:, b * LANES : (b + 1) * LANES] = block[:examples]
    each(dp_size, wait_score_sent)


def shards(sizes, hidden_in, out_grad, proj_in, proj_out, lengths, query_grads):
    dp_size, query_size, _ = sizes
    examples, seq, _ = hidden_in.shape
    rank = proj_in.shape[0]
    queries, flat = query_grads.shape
    planes = dp_size * query_size
    pieces = flat // LANES
    chunks = 4
    hbm = pl.BlockSpec(memory_space=pl.ANY)
    dma = pltpu.SemaphoreType.DMA
    sums = pltpu.VMEM((2, examples, rank, seq), jnp.float32)
    scores = pltpu.VMEM((dp_size, SUBLANES, LANES), jnp.float32)
    return pl.pallas_call(
        functools.partial(kernel, sizes, chunks),
        out_shape=jax.ShapeDtypeStruct((examples, dp_size * queries), jnp.float32),
        in_specs=[hbm, hbm, hbm, hbm, pl.BlockSpec(memory_space=pltpu.SMEM), hbm],
        out_specs=pl.BlockSpec(memory_space=pltpu.VMEM),
        scratch_shapes=[
            pltpu.VMEM(hidden_in.shape, hidden_in.dtype),
            pltpu.VMEM(out_grad.shape, out_grad.dtype),
            pltpu.VMEM(proj_in.shape, proj_in.dtype),
            pltpu.VMEM(proj_out.shape, proj_out.dtype),
            pltpu.VMEM(query_grads.shape, query_grads.dtype),
            sums,
            sums,
            pltpu.VMEM((planes, examples * pieces, LANES), jnp.float32),
            scores,
            scores,
            dma((3,)),
            dma((2, chunks)),
            dma((2,)),
            dma((2,)),
            dma((planes,)),
            dma((planes,)),
            dma((dp_size,)),
            dma((dp_size,)),
        ],
        compiler_params=pltpu.CompilerParams(
            collective_id=0, has_side_effects=True, vmem_limit_bytes=32 * 1024 * 1024
        ),
    )(hidden_in, out_grad, proj_in, proj_out, lengths, query_grads)


def solution(mesh):
    sizes = tuple(mesh.shape[a] for a in ("dp", "query", "mp"))
    in_specs = (
        P(("groups", "dp"), "query", "mp"),
        P(("groups", "dp"), "query", "mp"),
        P(None, "mp"),
        P(None, "mp"),
        P(("groups", "dp")),
        P(("groups", "query", "dp"), None),
    )
    out_specs = P(("groups", "dp"), "query")
    return jax.shard_map(
        functools.partial(shards, sizes),
        mesh=mesh,
        in_specs=in_specs,
        out_specs=out_specs,
        check_vma=False,
    )
```

```python
import functools

import jax
import jax.numpy as jnp
from jax import lax
from jax.experimental import pallas as pl
from jax.experimental.pallas import tpu as pltpu
from jax.sharding import PartitionSpec as P

DAMPING = 1.0
LANES = 128
SUBLANES = 8
MESH = pl.DeviceIdType.MESH
LAST = (((1,), (1,)), ((), ()))


def dot_last(left, right, precision=None):
    return lax.dot_general(
        left, right, LAST, precision=precision, preferred_element_type=jnp.float32
    )


def each(count, body):
    if count <= 16:
        for step in range(1, count):
            body(step)
    else:
        lax.fori_loop(1, count, lambda step, carry: (body(step), carry)[1], 0)


def solve_few(vectors, rhs, shift):
    total, width = rhs.shape
    rows = lax.broadcasted_iota(jnp.int32, (total, width), 0)
    columns = []
    for j in range(total):
        column = jnp.sum(vectors * vectors[j : j + 1], axis=1, keepdims=True)
        column = jnp.broadcast_to(column, (total, width))
        columns.append(jnp.where(rows == j, column + shift, column))
    for k in range(total):
        pivot = columns[k]
        inverse = 1.0 / pivot[k : k + 1]

        def step(array):
            own = array[k : k + 1] * inverse
            return jnp.where(rows == k, own, array - pivot * own)

        rhs = step(rhs)
        columns = [step(c) if j > k else c for j, c in enumerate(columns)]
    return rhs


def solve_many(vectors, rhs, shift):
    total, width = rhs.shape
    gram = dot_last(vectors, vectors, lax.Precision.HIGHEST)
    rows = lax.broadcasted_iota(jnp.int32, (total, total), 0)
    columns = lax.broadcasted_iota(jnp.int32, (total, total), 1)
    rhs_rows = lax.broadcasted_iota(jnp.int32, (total, width), 0)
    gram = jnp.where(rows == columns, gram + shift, gram)

    def step(k, carry):
        gram, rhs = carry
        column = jnp.sum(jnp.where(columns == k, gram, 0.0), axis=1, keepdims=True)
        row = jnp.sum(jnp.where(rows == k, gram, 0.0), axis=0, keepdims=True)
        rhs_row = jnp.sum(jnp.where(rhs_rows == k, rhs, 0.0), axis=0, keepdims=True)
        pivot = jnp.sum(
            jnp.where(columns[:1] == k, row, 0.0), axis=1, keepdims=True
        )
        row, rhs_row = row / pivot, rhs_row / pivot
        gram = jnp.where(rows == k, row, gram - column * row)
        rhs = jnp.where(rhs_rows == k, rhs_row, rhs - column * rhs_row)
        return gram, rhs

    return lax.fori_loop(0, total, step, (gram, rhs))[1]


def kernel(
    sizes,
    chunks,
    hidden_hbm,
    grad_hbm,
    proj_in_hbm,
    proj_out_hbm,
    lengths_hbm,
    query_hbm,
    out_ref,
    hidden,
    grad,
    proj_in,
    proj_out,
    lengths_ref,
    query,
    sums,
    pair,
    grads,
    sent,
    landed,
    load_sem,
    hidden_sem,
    pair_send,
    pair_recv,
    grads_send,
    grads_recv,
    score_send,
    score_recv,
):
    dp_size, query_size, mp_size = sizes
    assert mp_size == 2
    my_dp, my_query, my_mp = (lax.axis_index(a) for a in ("dp", "query", "mp"))
    other = 1 - my_mp
    examples, seq, width = hidden.shape
    rank = proj_in.shape[0]
    queries = query.shape[0]
    planes = dp_size * query_size
    me = my_query * dp_size + my_dp
    total = dp_size * examples
    repeat = LANES // rank
    pieces = rank // repeat
    step_width = width // chunks

    def load(source, target, sem):
        copy = pltpu.make_async_copy(source, target, sem)
        copy.start()
        return copy

    proj_out_copy = load(proj_out_hbm, proj_out, load_sem.at[0])
    grad_copy = load(grad_hbm, grad, load_sem.at[1])
    hidden_copies = []
    for c in range(chunks):
        part = pl.ds(c * step_width, step_width)
        hidden_copies.append(
            (
                load(proj_in_hbm.at[:, part], proj_in.at[:, part], hidden_sem.at[0, c]),
                load(hidden_hbm.at[:, :, part], hidden.at[:, :, part], hidden_sem.at[1, c]),
            )
        )
    query_copy = load(query_hbm, query, load_sem.at[2])
    lengths_copy = load(lengths_hbm, lengths_ref, load_sem.at[3])

    barrier = pltpu.get_barrier_semaphore()

    def place(step):
        slot = lax.rem(me + step, planes)
        return slot, {"dp": lax.rem(slot, dp_size), "query": slot // dp_size}

    def greet(step):
        pl.semaphore_signal(barrier, inc=1, device_id=place(step)[1], device_id_type=MESH)

    pl.semaphore_signal(barrier, inc=1, device_id={"mp": other}, device_id_type=MESH)
    each(planes, greet)

    proj_out_copy.wait()
    to_row = lax.broadcasted_iota(jnp.int32, (rank, rank), 0)
    from_row = lax.broadcasted_iota(jnp.int32, (rank, rank), 1)
    wanted = repeat * lax.rem(to_row, pieces) + to_row // pieces
    order = jnp.where(from_row == wanted, 1.0, 0.0).astype(jnp.bfloat16)
    ordered = jnp.dot(
        order, proj_out[...], preferred_element_type=jnp.float32
    ).astype(jnp.bfloat16)
    grad_copy.wait()
    for e in range(examples):
        sums[0, e] = dot_last(ordered, grad[e])

    pl.semaphore_wait(barrier, planes)

    def exchange(which):
        copy = pltpu.make_async_remote_copy(
            src_ref=sums.at[which],
            dst_ref=pair.at[which],
            send_sem=pair_send.at[which],
            recv_sem=pair_recv.at[which],
            device_id={"mp": other},
            device_id_type=MESH,
        )
        copy.start()
        return copy

    out_exchange = exchange(0)
    in_sums = [jnp.zeros((rank, seq), jnp.float32) for _ in range(examples)]
    for c in range(chunks):
        for copy in hidden_copies[c]:
            copy.wait()
        part = pl.ds(c * step_width, step_width)
        for e in range(examples):
            in_sums[e] += dot_last(proj_in[:, part], hidden[e, :, part])
    for e in range(examples):
        sums[1, e] = in_sums[e]
    query_copy.wait()
    lengths_copy.wait()
    in_exchange = exchange(1)
    out_exchange.wait()
    positions = my_query * seq + lax.broadcasted_iota(jnp.int32, (1, seq), 1)
    weighted = []
    for e in range(examples):
        used = jnp.full((1, seq), lengths_ref[e], jnp.int32)
        weights = jnp.where(positions < used, 1.0 / jnp.sqrt(used.astype(jnp.float32)), 0.0)
        weighted.append((sums[0, e] + pair[0, e]) * weights)
    in_exchange.wait()
    lanes = lax.broadcasted_iota(jnp.int32, (pieces, LANES), 1) // rank
    for e in range(examples):
        inputs = sums[1, e] + pair[1, e]
        product = dot_last(
            weighted[e], jnp.concatenate([inputs] * repeat, axis=0), lax.Precision.HIGHEST
        )
        flat = product[:pieces]
        for r in range(1, repeat):
            flat = jnp.where(lanes == r, product[r * pieces : (r + 1) * pieces], flat)
        grads[me, e * pieces : (e + 1) * pieces] = flat

    def grads_copy(slot, target):
        return pltpu.make_async_remote_copy(
            src_ref=grads.at[slot],
            dst_ref=grads.at[slot],
            send_sem=grads_send.at[target],
            recv_sem=grads_recv.at[slot],
            device_id=target_id(target),
            device_id_type=MESH,
        )

    def target_id(slot):
        return {"dp": lax.rem(slot, dp_size), "query": slot // dp_size}

    def send_grads(step):
        grads_copy(me, place(step)[0]).start()

    def wait_grads(step):
        slot = place(step)[0]
        grads_copy(slot, slot).wait_recv()

    def wait_sent(step):
        grads_copy(me, place(step)[0]).wait_send()

    each(planes, send_grads)
    each(planes, wait_grads)

    pieces_of = []
    flat_grads = grads.reshape(planes * examples * pieces, LANES)
    for p in range(pieces):
        piece = flat_grads[pl.ds(p, total, stride=pieces)]
        for q in range(1, query_size):
            piece += flat_grads[pl.ds(q * total * pieces + p, total, stride=pieces)]
        pieces_of.append(piece)
    vectors = jnp.concatenate(pieces_of, axis=1)
    blocks = LANES // queries
    rhs = dot_last(
        vectors, jnp.concatenate([query[...]] * blocks, axis=0), lax.Precision.HIGHEST
    )
    shift = DAMPING * total
    solve = solve_few if total <= SUBLANES else solve_many
    solved = solve(vectors, rhs * shift, shift)
    block_of_lane = lax.broadcasted_iota(jnp.int32, (total, LANES), 1) // queries
    solved = jnp.where(block_of_lane == lax.rem(my_dp, blocks), solved, 0.0)
    for d in range(dp_size):
        sent[d, :examples] = solved[d * examples : (d + 1) * examples]

    def score_copy(slot, target):
        return pltpu.make_async_remote_copy(
            src_ref=sent.at[target],
            dst_ref=landed.at[slot],
            send_sem=score_send.at[target],
            recv_sem=score_recv.at[slot],
            device_id={"dp": target},
            device_id_type=MESH,
        )

    def send_score(step):
        score_copy(my_dp, lax.rem(my_dp + step, dp_size)).start()

    def wait_score(step):
        slot = lax.rem(my_dp + step, dp_size)
        score_copy(slot, slot).wait_recv()

    def wait_score_sent(step):
        score_copy(my_dp, lax.rem(my_dp + step, dp_size)).wait_send()

    each(dp_size, send_score)
    landed[my_dp] = sent[my_dp]
    each(planes, wait_sent)
    each(dp_size, wait_score)
    for b in range(dp_size // blocks):
        block = landed[b * blocks]
        for d in range(b * blocks + 1, (b + 1) * blocks):
            block += landed[d]
        out_ref[:, b * LANES : (b + 1) * LANES] = block[:examples]
    each(dp_size, wait_score_sent)


def shards(sizes, hidden_in, out_grad, proj_in, proj_out, lengths, query_grads):
    dp_size, query_size, _ = sizes
    examples, seq, _ = hidden_in.shape
    rank = proj_in.shape[0]
    queries, flat = query_grads.shape
    planes = dp_size * query_size
    pieces = flat // LANES
    chunks = 4
    hbm = pl.BlockSpec(memory_space=pl.ANY)
    dma = pltpu.SemaphoreType.DMA
    sums = pltpu.VMEM((2, examples, rank, seq), jnp.float32)
    scores = pltpu.VMEM((dp_size, SUBLANES, LANES), jnp.float32)
    return pl.pallas_call(
        functools.partial(kernel, sizes, chunks),
        out_shape=jax.ShapeDtypeStruct((examples, dp_size * queries), jnp.float32),
        in_specs=[hbm, hbm, hbm, hbm, hbm, hbm],
        out_specs=pl.BlockSpec(memory_space=pltpu.VMEM),
        scratch_shapes=[
            pltpu.VMEM(hidden_in.shape, hidden_in.dtype),
            pltpu.VMEM(out_grad.shape, out_grad.dtype),
            pltpu.VMEM(proj_in.shape, proj_in.dtype),
            pltpu.VMEM(proj_out.shape, proj_out.dtype),
            pltpu.SMEM(lengths.shape, lengths.dtype),
            pltpu.VMEM(query_grads.shape, query_grads.dtype),
            sums,
            sums,
            pltpu.VMEM((planes, examples * pieces, LANES), jnp.float32),
            scores,
            scores,
            dma((4,)),
            dma((2, chunks)),
            dma((2,)),
            dma((2,)),
            dma((planes,)),
            dma((planes,)),
            dma((dp_size,)),
            dma((dp_size,)),
        ],
        compiler_params=pltpu.CompilerParams(
            collective_id=0, has_side_effects=True, vmem_limit_bytes=32 * 1024 * 1024
        ),
    )(*(pltpu.with_memory_space_constraint(a, pltpu.HBM) for a in (hidden_in, out_grad, proj_in, proj_out, lengths, query_grads)))


def solution(mesh):
    sizes = tuple(mesh.shape[a] for a in ("dp", "query", "mp"))
    in_specs = (
        P(("groups", "dp"), "query", "mp"),
        P(("groups", "dp"), "query", "mp"),
        P(None, "mp"),
        P(None, "mp"),
        P(("groups", "dp")),
        P(("groups", "query", "dp"), None),
    )
    out_specs = P(("groups", "dp"), "query")
    return jax.shard_map(
        functools.partial(shards, sizes),
        mesh=mesh,
        in_specs=in_specs,
        out_specs=out_specs,
        check_vma=False,
    )
```

```python
import functools

import jax
import jax.numpy as jnp
from jax import lax
from jax.experimental import pallas as pl
from jax.experimental.pallas import tpu as pltpu
from jax.sharding import PartitionSpec as P

DAMPING = 1.0
LANES = 128
SUBLANES = 8
MESH = pl.DeviceIdType.MESH
LAST = (((1,), (1,)), ((), ()))


def dot_last(left, right, precision=None):
    return lax.dot_general(
        left, right, LAST, precision=precision, preferred_element_type=jnp.float32
    )


def each(count, body):
    if count <= 16:
        for step in range(1, count):
            body(step)
    else:
        lax.fori_loop(1, count, lambda step, carry: (body(step), carry)[1], 0)


def solve_few(vectors, rhs, shift):
    total, width = rhs.shape
    rows = lax.broadcasted_iota(jnp.int32, (total, LANES), 0)
    columns = []
    parts = [rhs[:, at : at + LANES] for at in range(0, width, LANES)]
    for j in range(total):
        column = jnp.sum(vectors * vectors[j : j + 1], axis=1, keepdims=True)
        column = jnp.broadcast_to(column, (total, LANES))
        columns.append(jnp.where(rows == j, column + shift, column))
    for k in range(total):
        pivot = columns[k]
        inverse = 1.0 / pivot[k : k + 1]

        def step(array):
            own = array[k : k + 1] * inverse
            return jnp.where(rows == k, own, array - pivot * own)

        parts = [step(part) for part in parts]
        columns = [step(c) if j > k else c for j, c in enumerate(columns)]
    return jnp.concatenate(parts, axis=1)


def solve_many(vectors, rhs, shift):
    total, width = rhs.shape
    gram = dot_last(vectors, vectors, lax.Precision.HIGHEST)
    rows = lax.broadcasted_iota(jnp.int32, (total, total), 0)
    columns = lax.broadcasted_iota(jnp.int32, (total, total), 1)
    rhs_rows = lax.broadcasted_iota(jnp.int32, (total, width), 0)
    gram = jnp.where(rows == columns, gram + shift, gram)

    def step(k, carry):
        gram, rhs = carry
        column = jnp.sum(jnp.where(columns == k, gram, 0.0), axis=1, keepdims=True)
        row = jnp.sum(jnp.where(rows == k, gram, 0.0), axis=0, keepdims=True)
        rhs_row = jnp.sum(jnp.where(rhs_rows == k, rhs, 0.0), axis=0, keepdims=True)
        pivot = jnp.sum(
            jnp.where(columns[:1] == k, row, 0.0), axis=1, keepdims=True
        )
        row, rhs_row = row / pivot, rhs_row / pivot
        gram = jnp.where(rows == k, row, gram - column * row)
        rhs = jnp.where(rhs_rows == k, rhs_row, rhs - column * rhs_row)
        return gram, rhs

    return lax.fori_loop(0, total, step, (gram, rhs))[1]


def kernel(
    sizes,
    chunks,
    hidden_hbm,
    grad_hbm,
    proj_in_hbm,
    proj_out_hbm,
    lengths_hbm,
    query_hbm,
    out_ref,
    hidden,
    grad,
    proj_in,
    proj_out,
    lengths_ref,
    query,
    sums,
    pair,
    grads,
    sent,
    landed,
    load_sem,
    hidden_sem,
    pair_send,
    pair_recv,
    grads_send,
    grads_recv,
    score_send,
    score_recv,
    query_send,
    query_recv,
    share_send,
    share_recv,
):
    dp_size, query_size, mp_size = sizes
    assert mp_size == 2
    my_dp, my_query, my_mp = (lax.axis_index(a) for a in ("dp", "query", "mp"))
    other = 1 - my_mp
    examples, seq, width = hidden.shape
    rank = proj_in.shape[0]
    gathered = query.shape[0] == dp_size
    queries = query.shape[1] * query.shape[2]
    features = query.shape[3]
    planes = dp_size * query_size
    me = my_query * dp_size + my_dp
    total = dp_size * examples
    repeat = LANES // rank
    pieces = rank // repeat
    step_width = width // chunks

    def load(source, target, sem):
        copy = pltpu.make_async_copy(source, target, sem)
        copy.start()
        return copy

    proj_out_copy = load(proj_out_hbm, proj_out, load_sem.at[0])
    grad_copy = load(grad_hbm, grad, load_sem.at[1])
    hidden_copies = []
    for c in range(chunks):
        part = pl.ds(c * step_width, step_width)
        hidden_copies.append(
            (
                load(proj_in_hbm.at[:, part], proj_in.at[:, part], hidden_sem.at[0, c]),
                load(hidden_hbm.at[:, :, part], hidden.at[:, :, part], hidden_sem.at[1, c]),
            )
        )
    own_query = my_dp if gathered else 0
    query_copy = load(query_hbm, query.at[own_query], load_sem.at[2])
    lengths_copy = load(lengths_hbm, lengths_ref, load_sem.at[3])

    barrier = pltpu.get_barrier_semaphore()

    def place(step):
        slot = lax.rem(me + step, planes)
        return slot, {"dp": lax.rem(slot, dp_size), "query": slot // dp_size}

    def greet(step):
        pl.semaphore_signal(barrier, inc=1, device_id=place(step)[1], device_id_type=MESH)

    pl.semaphore_signal(barrier, inc=1, device_id={"mp": other}, device_id_type=MESH)
    each(planes, greet)

    proj_out_copy.wait()
    to_row = lax.broadcasted_iota(jnp.int32, (rank, rank), 0)
    from_row = lax.broadcasted_iota(jnp.int32, (rank, rank), 1)
    wanted = repeat * lax.rem(to_row, pieces) + to_row // pieces
    order = jnp.where(from_row == wanted, 1.0, 0.0).astype(jnp.bfloat16)
    ordered = jnp.dot(
        order, proj_out[...], preferred_element_type=jnp.float32
    ).astype(jnp.bfloat16)
    grad_copy.wait()
    for e in range(examples):
        sums[0, e] = dot_last(grad[e], ordered).T

    pl.semaphore_wait(barrier, planes)

    def exchange(which):
        copy = pltpu.make_async_remote_copy(
            src_ref=sums.at[which],
            dst_ref=pair.at[which],
            send_sem=pair_send.at[which],
            recv_sem=pair_recv.at[which],
            device_id={"mp": other},
            device_id_type=MESH,
        )
        copy.start()
        return copy

    def query_to(slot, target):
        return pltpu.make_async_remote_copy(
            src_ref=query_hbm.at[my_mp],
            dst_ref=query.at[slot, my_mp],
            send_sem=query_send.at[target],
            recv_sem=query_recv.at[slot],
            device_id={"dp": target},
            device_id_type=MESH,
        )

    def query_share(slot, half):
        return pltpu.make_async_remote_copy(
            src_ref=query.at[slot, half],
            dst_ref=query.at[slot, half],
            send_sem=share_send.at[slot],
            recv_sem=share_recv.at[slot],
            device_id={"mp": other},
            device_id_type=MESH,
        )

    def dp_slot(step):
        return lax.rem(my_dp + step, dp_size)

    out_exchange = exchange(0)
    if gathered:
        each(dp_size, lambda step: query_to(my_dp, dp_slot(step)).start())
    in_sums = [jnp.zeros((seq, rank), jnp.float32) for _ in range(examples)]
    for c in range(chunks):
        for copy in hidden_copies[c]:
            copy.wait()
        part = pl.ds(c * step_width, step_width)
        for e in range(examples):
            in_sums[e] += dot_last(hidden[e, :, part], proj_in[:, part])
    for e in range(examples):
        sums[1, e] = in_sums[e].T
    query_copy.wait()
    lengths_copy.wait()
    in_exchange = exchange(1)
    out_exchange.wait()
    positions = my_query * seq + lax.broadcasted_iota(jnp.int32, (1, seq), 1)
    weighted = []
    for e in range(examples):
        used = jnp.full((1, seq), lengths_ref[e], jnp.int32)
        weights = jnp.where(positions < used, 1.0 / jnp.sqrt(used.astype(jnp.float32)), 0.0)
        weighted.append((sums[0, e] + pair[0, e]) * weights)
    in_exchange.wait()
    lanes = lax.broadcasted_iota(jnp.int32, (pieces, LANES), 1) // rank
    for e in range(examples):
        inputs = sums[1, e] + pair[1, e]
        product = dot_last(
            weighted[e], jnp.concatenate([inputs] * repeat, axis=0), lax.Precision.HIGHEST
        )
        flat = product[:pieces]
        for r in range(1, repeat):
            flat = jnp.where(lanes == r, product[r * pieces : (r + 1) * pieces], flat)
        grads[me, e * pieces : (e + 1) * pieces] = flat

    def grads_copy(slot, target):
        return pltpu.make_async_remote_copy(
            src_ref=grads.at[slot],
            dst_ref=grads.at[slot],
            send_sem=grads_send.at[target],
            recv_sem=grads_recv.at[slot],
            device_id=target_id(target),
            device_id_type=MESH,
        )

    def target_id(slot):
        return {"dp": lax.rem(slot, dp_size), "query": slot // dp_size}

    def send_grads(step):
        grads_copy(me, place(step)[0]).start()

    def wait_grads(step):
        slot = place(step)[0]
        grads_copy(slot, slot).wait_recv()

    def wait_sent(step):
        grads_copy(me, place(step)[0]).wait_send()

    each(planes, send_grads)
    if gathered:
        for step in range(1, dp_size):
            slot = dp_slot(step)
            query_to(slot, slot).wait_recv()
            query_share(slot, my_mp).start()
    each(planes, wait_grads)

    pieces_of = []
    flat_grads = grads.reshape(planes * examples * pieces, LANES)
    for p in range(pieces):
        piece = flat_grads[pl.ds(p, total, stride=pieces)]
        for q in range(1, query_size):
            piece += flat_grads[pl.ds(q * total * pieces + p, total, stride=pieces)]
        pieces_of.append(piece)
    vectors = jnp.concatenate(pieces_of, axis=1)
    blocks = LANES // queries
    shift = DAMPING * total
    solve = solve_few if total <= SUBLANES else solve_many
    if gathered:
        solved = solve(vectors, vectors * shift, shift)
        for step in range(1, dp_size):
            query_share(dp_slot(step), other).wait_recv()
        scores = dot_last(
            solved, query[...].reshape(dp_size * queries, features), lax.Precision.HIGHEST
        )
        mine = scores[:examples]
        for d in range(1, dp_size):
            mine = jnp.where(my_dp == d, scores[d * examples : (d + 1) * examples], mine)
        out_ref[...] = mine
        each(planes, wait_sent)
        for step in range(1, dp_size):
            query_to(my_dp, dp_slot(step)).wait_send()
            query_share(dp_slot(step), my_mp).wait_send()
        return
    rhs = dot_last(
        vectors, jnp.concatenate([query[0].reshape(queries, features)] * blocks, axis=0), lax.Precision.HIGHEST
    )
    solved = solve(vectors, rhs * shift, shift)
    block_of_lane = lax.broadcasted_iota(jnp.int32, (total, LANES), 1) // queries
    solved = jnp.where(block_of_lane == lax.rem(my_dp, blocks), solved, 0.0)
    for d in range(dp_size):
        sent[d, :examples] = solved[d * examples : (d + 1) * examples]

    def score_copy(slot, target):
        return pltpu.make_async_remote_copy(
            src_ref=sent.at[target],
            dst_ref=landed.at[slot],
            send_sem=score_send.at[target],
            recv_sem=score_recv.at[slot],
            device_id={"dp": target},
            device_id_type=MESH,
        )

    def send_score(step):
        score_copy(my_dp, lax.rem(my_dp + step, dp_size)).start()

    def wait_score(step):
        slot = lax.rem(my_dp + step, dp_size)
        score_copy(slot, slot).wait_recv()

    def wait_score_sent(step):
        score_copy(my_dp, lax.rem(my_dp + step, dp_size)).wait_send()

    each(dp_size, send_score)
    landed[my_dp] = sent[my_dp]
    each(planes, wait_sent)
    each(dp_size, wait_score)
    for b in range(dp_size // blocks):
        block = landed[b * blocks]
        for d in range(b * blocks + 1, (b + 1) * blocks):
            block += landed[d]
        out_ref[:, b * LANES : (b + 1) * LANES] = block[:examples]
    each(dp_size, wait_score_sent)


def shards(sizes, hidden_in, out_grad, proj_in, proj_out, lengths, query_grads):
    dp_size, query_size, mp_size = sizes
    examples, seq, _ = hidden_in.shape
    rank = proj_in.shape[0]
    queries, flat = query_grads.shape
    query_grads = query_grads.reshape(mp_size, queries // mp_size, flat)
    held = dp_size if dp_size <= 4 else 1
    planes = dp_size * query_size
    pieces = flat // LANES
    chunks = 4
    hbm = pl.BlockSpec(memory_space=pl.ANY)
    dma = pltpu.SemaphoreType.DMA
    sums = pltpu.VMEM((2, examples, rank, seq), jnp.float32)
    scores = pltpu.VMEM((dp_size, SUBLANES, LANES), jnp.float32)
    return pl.pallas_call(
        functools.partial(kernel, sizes, chunks),
        out_shape=jax.ShapeDtypeStruct((examples, dp_size * queries), jnp.float32),
        in_specs=[hbm, hbm, hbm, hbm, hbm, hbm],
        out_specs=pl.BlockSpec(memory_space=pltpu.VMEM),
        scratch_shapes=[
            pltpu.VMEM(hidden_in.shape, hidden_in.dtype),
            pltpu.VMEM(out_grad.shape, out_grad.dtype),
            pltpu.VMEM(proj_in.shape, proj_in.dtype),
            pltpu.VMEM(proj_out.shape, proj_out.dtype),
            pltpu.SMEM(lengths.shape, lengths.dtype),
            pltpu.VMEM((held, *query_grads.shape), query_grads.dtype),
            sums,
            sums,
            pltpu.VMEM((planes, examples * pieces, LANES), jnp.float32),
            scores,
            scores,
            dma((4,)),
            dma((2, chunks)),
            dma((2,)),
            dma((2,)),
            dma((planes,)),
            dma((planes,)),
            dma((dp_size,)),
            dma((dp_size,)),
            dma((held,)),
            dma((held,)),
            dma((held,)),
            dma((held,)),
        ],
        compiler_params=pltpu.CompilerParams(
            collective_id=0, has_side_effects=True, vmem_limit_bytes=32 * 1024 * 1024
        ),
    )(*(pltpu.with_memory_space_constraint(a, pltpu.HBM) for a in (hidden_in, out_grad, proj_in, proj_out, lengths, query_grads)))


def solution(mesh):
    sizes = tuple(mesh.shape[a] for a in ("dp", "query", "mp"))
    in_specs = (
        P(("groups", "dp"), "query", "mp"),
        P(("groups", "dp"), "query", "mp"),
        P(None, "mp"),
        P(None, "mp"),
        P(("groups", "dp")),
        P(("groups", "query", "dp"), None),
    )
    out_specs = P(("groups", "dp"), "query")
    return jax.shard_map(
        functools.partial(shards, sizes),
        mesh=mesh,
        in_specs=in_specs,
        out_specs=out_specs,
        check_vma=False,
    )
```

```python
import functools

import jax
import jax.numpy as jnp
from jax import lax
from jax.experimental import pallas as pl
from jax.experimental.pallas import tpu as pltpu
from jax.sharding import PartitionSpec as P

DAMPING = 1.0
LANES = 128
SUBLANES = 8
MESH = pl.DeviceIdType.MESH
LAST = (((1,), (1,)), ((), ()))


def dot_last(left, right, precision=None):
    return lax.dot_general(
        left, right, LAST, precision=precision, preferred_element_type=jnp.float32
    )


def dot_split(left, right):
    lefts, rights = [], []
    for array, parts in ((left, lefts), (right, rights)):
        high = array.astype(jnp.bfloat16)
        parts += [high, (array - high.astype(jnp.float32)).astype(jnp.bfloat16)]
    rows = left.shape[0]
    both = dot_last(jnp.concatenate(lefts, axis=0), rights[0])
    return both[:rows] + (both[rows:] + dot_last(lefts[0], rights[1]))


def each(count, body):
    if count <= 16:
        for step in range(1, count):
            body(step)
    else:
        lax.fori_loop(1, count, lambda step, carry: (body(step), carry)[1], 0)


def solve_few(vectors, rhs, shift):
    total, width = rhs.shape
    rows = lax.broadcasted_iota(jnp.int32, (total, LANES), 0)
    columns = []
    parts = [rhs[:, at : at + LANES] for at in range(0, width, LANES)]
    for j in range(total):
        column = jnp.sum(vectors * vectors[j : j + 1], axis=1, keepdims=True)
        column = jnp.broadcast_to(column, (total, LANES))
        columns.append(jnp.where(rows == j, column + shift, column))
    for k in range(total):
        pivot = columns[k]
        inverse = 1.0 / pivot[k : k + 1]

        def step(array):
            own = array[k : k + 1] * inverse
            return jnp.where(rows == k, own, array - pivot * own)

        parts = [step(part) for part in parts]
        columns = [step(c) if j > k else c for j, c in enumerate(columns)]
    return jnp.concatenate(parts, axis=1)


def solve_many(vectors, rhs, shift):
    total, width = rhs.shape
    gram = dot_last(vectors, vectors, lax.Precision.HIGHEST)
    rows = lax.broadcasted_iota(jnp.int32, (total, total), 0)
    columns = lax.broadcasted_iota(jnp.int32, (total, total), 1)
    rhs_rows = lax.broadcasted_iota(jnp.int32, (total, width), 0)
    gram = jnp.where(rows == columns, gram + shift, gram)

    def step(k, carry):
        gram, rhs = carry
        column = jnp.sum(jnp.where(columns == k, gram, 0.0), axis=1, keepdims=True)
        row = jnp.sum(jnp.where(rows == k, gram, 0.0), axis=0, keepdims=True)
        rhs_row = jnp.sum(jnp.where(rhs_rows == k, rhs, 0.0), axis=0, keepdims=True)
        pivot = jnp.sum(
            jnp.where(columns[:1] == k, row, 0.0), axis=1, keepdims=True
        )
        row, rhs_row = row / pivot, rhs_row / pivot
        gram = jnp.where(rows == k, row, gram - column * row)
        rhs = jnp.where(rhs_rows == k, rhs_row, rhs - column * rhs_row)
        return gram, rhs

    return lax.fori_loop(0, total, step, (gram, rhs))[1]


def kernel(
    sizes,
    chunks,
    hidden_hbm,
    grad_hbm,
    proj_in_hbm,
    proj_out_hbm,
    lengths_hbm,
    query_hbm,
    out_ref,
    hidden,
    grad,
    proj_in,
    proj_out,
    lengths_ref,
    query,
    sums,
    pair,
    grads,
    sent,
    landed,
    load_sem,
    hidden_sem,
    pair_send,
    pair_recv,
    grads_send,
    grads_recv,
    score_send,
    score_recv,
    query_send,
    query_recv,
    share_send,
    share_recv,
):
    dp_size, query_size, mp_size = sizes
    assert mp_size == 2
    my_dp, my_query, my_mp = (lax.axis_index(a) for a in ("dp", "query", "mp"))
    other = 1 - my_mp
    examples, seq, width = hidden.shape
    rank = proj_in.shape[0]
    gathered = query.shape[0] == dp_size
    queries = query.shape[1] * query.shape[2]
    features = query.shape[3]
    planes = dp_size * query_size
    me = my_query * dp_size + my_dp
    total = dp_size * examples
    repeat = LANES // rank
    pieces = rank // repeat
    step_width = width // chunks

    def load(source, target, sem):
        copy = pltpu.make_async_copy(source, target, sem)
        copy.start()
        return copy

    proj_out_copy = load(proj_out_hbm, proj_out, load_sem.at[0])
    grad_copy = load(grad_hbm, grad, load_sem.at[1])
    hidden_copies = []
    for c in range(chunks):
        part = pl.ds(c * step_width, step_width)
        hidden_copies.append(
            (
                load(proj_in_hbm.at[:, part], proj_in.at[:, part], hidden_sem.at[0, c]),
                load(hidden_hbm.at[:, :, part], hidden.at[:, :, part], hidden_sem.at[1, c]),
            )
        )
    own_query = my_dp if gathered else 0
    query_copy = load(query_hbm, query.at[own_query], load_sem.at[2])
    lengths_copy = load(lengths_hbm, lengths_ref, load_sem.at[3])

    barrier = pltpu.get_barrier_semaphore()

    def place(step):
        slot = lax.rem(me + step, planes)
        return slot, {"dp": lax.rem(slot, dp_size), "query": slot // dp_size}

    def greet(step):
        pl.semaphore_signal(barrier, inc=1, device_id=place(step)[1], device_id_type=MESH)

    pl.semaphore_signal(barrier, inc=1, device_id={"mp": other}, device_id_type=MESH)
    each(planes, greet)

    pl.semaphore_wait(barrier, planes)

    def exchange(which):
        copy = pltpu.make_async_remote_copy(
            src_ref=sums.at[which],
            dst_ref=pair.at[which],
            send_sem=pair_send.at[which],
            recv_sem=pair_recv.at[which],
            device_id={"mp": other},
            device_id_type=MESH,
        )
        copy.start()
        return copy

    def query_to(slot, target):
        return pltpu.make_async_remote_copy(
            src_ref=query_hbm.at[my_mp],
            dst_ref=query.at[slot, my_mp],
            send_sem=query_send.at[target],
            recv_sem=query_recv.at[slot],
            device_id={"dp": target},
            device_id_type=MESH,
        )

    def query_share(slot, half):
        return pltpu.make_async_remote_copy(
            src_ref=query.at[slot, half],
            dst_ref=query.at[slot, half],
            send_sem=share_send.at[slot],
            recv_sem=share_recv.at[slot],
            device_id={"mp": other},
            device_id_type=MESH,
        )

    def dp_slot(step):
        return lax.rem(my_dp + step, dp_size)

    if gathered:
        each(dp_size, lambda step: query_to(my_dp, dp_slot(step)).start())

    proj_out_copy.wait()
    to_row = lax.broadcasted_iota(jnp.int32, (rank, rank), 0)
    from_row = lax.broadcasted_iota(jnp.int32, (rank, rank), 1)
    wanted = repeat * lax.rem(to_row, pieces) + to_row // pieces
    order = jnp.where(from_row == wanted, 1.0, 0.0).astype(jnp.bfloat16)
    ordered = jnp.dot(
        order, proj_out[...], preferred_element_type=jnp.float32
    ).astype(jnp.bfloat16)
    grad_copy.wait()
    for e in range(examples):
        sums[0, e] = dot_last(grad[e], ordered).T

    out_exchange = exchange(0)
    in_sums = [jnp.zeros((seq, rank), jnp.float32) for _ in range(examples)]
    for c in range(chunks):
        for copy in hidden_copies[c]:
            copy.wait()
        part = pl.ds(c * step_width, step_width)
        for e in range(examples):
            in_sums[e] += dot_last(hidden[e, :, part], proj_in[:, part])
    for e in range(examples):
        sums[1, e] = in_sums[e].T
    query_copy.wait()
    lengths_copy.wait()
    in_exchange = exchange(1)
    out_exchange.wait()
    positions = my_query * seq + lax.broadcasted_iota(jnp.int32, (1, seq), 1)
    weighted = []
    for e in range(examples):
        used = jnp.full((1, seq), lengths_ref[e], jnp.int32)
        weights = jnp.where(positions < used, 1.0 / jnp.sqrt(used.astype(jnp.float32)), 0.0)
        weighted.append((sums[0, e] + pair[0, e]) * weights)
    in_exchange.wait()
    lanes = lax.broadcasted_iota(jnp.int32, (pieces, LANES), 1) // rank
    for e in range(examples):
        inputs = sums[1, e] + pair[1, e]
        product = dot_last(
            weighted[e], jnp.concatenate([inputs] * repeat, axis=0), lax.Precision.HIGHEST
        )
        flat = product[:pieces]
        for r in range(1, repeat):
            flat = jnp.where(lanes == r, product[r * pieces : (r + 1) * pieces], flat)
        grads[me, e * pieces : (e + 1) * pieces] = flat

    def grads_copy(slot, target):
        return pltpu.make_async_remote_copy(
            src_ref=grads.at[slot],
            dst_ref=grads.at[slot],
            send_sem=grads_send.at[target],
            recv_sem=grads_recv.at[slot],
            device_id=target_id(target),
            device_id_type=MESH,
        )

    def target_id(slot):
        return {"dp": lax.rem(slot, dp_size), "query": slot // dp_size}

    def send_grads(step):
        grads_copy(me, place(step)[0]).start()

    def wait_grads(step):
        slot = place(step)[0]
        grads_copy(slot, slot).wait_recv()

    def wait_sent(step):
        grads_copy(me, place(step)[0]).wait_send()

    each(planes, send_grads)
    if gathered:
        for step in range(1, dp_size):
            slot = dp_slot(step)
            query_to(slot, slot).wait_recv()
            query_share(slot, my_mp).start()
    each(planes, wait_grads)

    pieces_of = []
    flat_grads = grads.reshape(planes * examples * pieces, LANES)
    for p in range(pieces):
        piece = flat_grads[pl.ds(p, total, stride=pieces)]
        for q in range(1, query_size):
            piece += flat_grads[pl.ds(q * total * pieces + p, total, stride=pieces)]
        pieces_of.append(piece)
    vectors = jnp.concatenate(pieces_of, axis=1)
    blocks = LANES // queries
    shift = DAMPING * total
    solve = solve_few if total <= SUBLANES else solve_many
    if gathered:
        solved = solve(vectors, vectors * shift, shift)
        for step in range(1, dp_size):
            query_share(dp_slot(step), other).wait_recv()
        scores = dot_split(solved, query[...].reshape(dp_size * queries, features))
        mine = scores[:examples]
        for d in range(1, dp_size):
            mine = jnp.where(my_dp == d, scores[d * examples : (d + 1) * examples], mine)
        out_ref[...] = mine
        each(planes, wait_sent)
        for step in range(1, dp_size):
            query_to(my_dp, dp_slot(step)).wait_send()
            query_share(dp_slot(step), my_mp).wait_send()
        return
    rhs = dot_last(
        vectors, jnp.concatenate([query[0].reshape(queries, features)] * blocks, axis=0), lax.Precision.HIGHEST
    )
    solved = solve(vectors, rhs * shift, shift)
    block_of_lane = lax.broadcasted_iota(jnp.int32, (total, LANES), 1) // queries
    solved = jnp.where(block_of_lane == lax.rem(my_dp, blocks), solved, 0.0)
    for d in range(dp_size):
        sent[d, :examples] = solved[d * examples : (d + 1) * examples]

    def score_copy(slot, target):
        return pltpu.make_async_remote_copy(
            src_ref=sent.at[target],
            dst_ref=landed.at[slot],
            send_sem=score_send.at[target],
            recv_sem=score_recv.at[slot],
            device_id={"dp": target},
            device_id_type=MESH,
        )

    def send_score(step):
        score_copy(my_dp, lax.rem(my_dp + step, dp_size)).start()

    def wait_score(step):
        slot = lax.rem(my_dp + step, dp_size)
        score_copy(slot, slot).wait_recv()

    def wait_score_sent(step):
        score_copy(my_dp, lax.rem(my_dp + step, dp_size)).wait_send()

    each(dp_size, send_score)
    landed[my_dp] = sent[my_dp]
    each(planes, wait_sent)
    each(dp_size, wait_score)
    for b in range(dp_size // blocks):
        block = landed[b * blocks]
        for d in range(b * blocks + 1, (b + 1) * blocks):
            block += landed[d]
        out_ref[:, b * LANES : (b + 1) * LANES] = block[:examples]
    each(dp_size, wait_score_sent)


def shards(sizes, hidden_in, out_grad, proj_in, proj_out, lengths, query_grads):
    dp_size, query_size, mp_size = sizes
    examples, seq, _ = hidden_in.shape
    rank = proj_in.shape[0]
    queries, flat = query_grads.shape
    query_grads = query_grads.reshape(mp_size, queries // mp_size, flat)
    held = dp_size if dp_size <= 4 else 1
    planes = dp_size * query_size
    pieces = flat // LANES
    chunks = 4
    hbm = pl.BlockSpec(memory_space=pl.ANY)
    dma = pltpu.SemaphoreType.DMA
    sums = pltpu.VMEM((2, examples, rank, seq), jnp.float32)
    scores = pltpu.VMEM((dp_size, SUBLANES, LANES), jnp.float32)
    return pl.pallas_call(
        functools.partial(kernel, sizes, chunks),
        out_shape=jax.ShapeDtypeStruct((examples, dp_size * queries), jnp.float32),
        in_specs=[hbm, hbm, hbm, hbm, hbm, hbm],
        out_specs=pl.BlockSpec(memory_space=pltpu.VMEM),
        scratch_shapes=[
            pltpu.VMEM(hidden_in.shape, hidden_in.dtype),
            pltpu.VMEM(out_grad.shape, out_grad.dtype),
            pltpu.VMEM(proj_in.shape, proj_in.dtype),
            pltpu.VMEM(proj_out.shape, proj_out.dtype),
            pltpu.SMEM(lengths.shape, lengths.dtype),
            pltpu.VMEM((held, *query_grads.shape), query_grads.dtype),
            sums,
            sums,
            pltpu.VMEM((planes, examples * pieces, LANES), jnp.float32),
            scores,
            scores,
            dma((4,)),
            dma((2, chunks)),
            dma((2,)),
            dma((2,)),
            dma((planes,)),
            dma((planes,)),
            dma((dp_size,)),
            dma((dp_size,)),
            dma((held,)),
            dma((held,)),
            dma((held,)),
            dma((held,)),
        ],
        compiler_params=pltpu.CompilerParams(
            collective_id=0, has_side_effects=True, vmem_limit_bytes=32 * 1024 * 1024
        ),
    )(*(pltpu.with_memory_space_constraint(a, pltpu.HBM) for a in (hidden_in, out_grad, proj_in, proj_out, lengths, query_grads)))


def solution(mesh):
    sizes = tuple(mesh.shape[a] for a in ("dp", "query", "mp"))
    in_specs = (
        P(("groups", "dp"), "query", "mp"),
        P(("groups", "dp"), "query", "mp"),
        P(None, "mp"),
        P(None, "mp"),
        P(("groups", "dp")),
        P(("groups", "query", "dp"), None),
    )
    out_specs = P(("groups", "dp"), "query")
    return jax.shard_map(
        functools.partial(shards, sizes),
        mesh=mesh,
        in_specs=in_specs,
        out_specs=out_specs,
        check_vma=False,
    )
```

```python
import functools

import jax
import jax.numpy as jnp
from jax import lax
from jax.experimental import pallas as pl
from jax.experimental.pallas import tpu as pltpu
from jax.sharding import PartitionSpec as P

DAMPING = 1.0
LANES = 128
SUBLANES = 8
MESH = pl.DeviceIdType.MESH
LAST = (((1,), (1,)), ((), ()))


def dot_last(left, right, precision=None):
    return lax.dot_general(
        left, right, LAST, precision=precision, preferred_element_type=jnp.float32
    )


def dot_split(left, right):
    lefts, rights = [], []
    for array, parts in ((left, lefts), (right, rights)):
        high = array.astype(jnp.bfloat16)
        parts += [high, (array - high.astype(jnp.float32)).astype(jnp.bfloat16)]
    rows = left.shape[0]
    both = dot_last(jnp.concatenate(lefts, axis=0), rights[0])
    return both[:rows] + (both[rows:] + dot_last(lefts[0], rights[1]))


def each(count, body):
    if count <= 16:
        for step in range(1, count):
            body(step)
    else:
        lax.fori_loop(1, count, lambda step, carry: (body(step), carry)[1], 0)


def solve_few(vectors, rhs, shift):
    total, width = rhs.shape
    rows = lax.broadcasted_iota(jnp.int32, (total, LANES), 0)
    columns = []
    parts = [rhs[:, at : at + LANES] for at in range(0, width, LANES)]
    for j in range(total):
        column = jnp.sum(vectors * vectors[j : j + 1], axis=1, keepdims=True)
        column = jnp.broadcast_to(column, (total, LANES))
        columns.append(jnp.where(rows == j, column + shift, column))
    for k in range(total):
        pivot = columns[k]
        inverse = 1.0 / pivot[k : k + 1]

        def step(array):
            own = array[k : k + 1] * inverse
            return jnp.where(rows == k, own, array - pivot * own)

        parts = [step(part) for part in parts]
        columns = [step(c) if j > k else c for j, c in enumerate(columns)]
    return jnp.concatenate(parts, axis=1)


def solve_many(vectors, rhs, shift):
    total, width = rhs.shape
    gram = dot_last(vectors, vectors, lax.Precision.HIGHEST)
    rows = lax.broadcasted_iota(jnp.int32, (total, total), 0)
    columns = lax.broadcasted_iota(jnp.int32, (total, total), 1)
    rhs_rows = lax.broadcasted_iota(jnp.int32, (total, width), 0)
    gram = jnp.where(rows == columns, gram + shift, gram)

    def step(k, carry):
        gram, rhs = carry
        column = jnp.sum(jnp.where(columns == k, gram, 0.0), axis=1, keepdims=True)
        row = jnp.sum(jnp.where(rows == k, gram, 0.0), axis=0, keepdims=True)
        rhs_row = jnp.sum(jnp.where(rhs_rows == k, rhs, 0.0), axis=0, keepdims=True)
        pivot = jnp.sum(
            jnp.where(columns[:1] == k, row, 0.0), axis=1, keepdims=True
        )
        row, rhs_row = row / pivot, rhs_row / pivot
        gram = jnp.where(rows == k, row, gram - column * row)
        rhs = jnp.where(rhs_rows == k, rhs_row, rhs - column * rhs_row)
        return gram, rhs

    return lax.fori_loop(0, total, step, (gram, rhs))[1]


def kernel(
    sizes,
    chunks,
    hidden_hbm,
    grad_hbm,
    proj_in_hbm,
    proj_out_hbm,
    lengths_hbm,
    query_hbm,
    out_ref,
    hidden,
    grad,
    proj_in,
    proj_out,
    lengths_ref,
    query,
    sums,
    pair,
    grads,
    sent,
    landed,
    load_sem,
    hidden_sem,
    pair_send,
    pair_recv,
    grads_send,
    grads_recv,
    score_send,
    score_recv,
    query_send,
    query_recv,
    share_send,
    share_recv,
):
    dp_size, query_size, mp_size = sizes
    assert mp_size == 2
    my_dp, my_query, my_mp = (lax.axis_index(a) for a in ("dp", "query", "mp"))
    other = 1 - my_mp
    examples, seq, width = hidden.shape
    rank = proj_in.shape[0]
    gathered = query.shape[0] == dp_size == 4
    queries = query.shape[1] * query.shape[2] * query.shape[3]
    features = query.shape[4]
    planes = dp_size * query_size
    me = my_query * dp_size + my_dp
    total = dp_size * examples
    repeat = LANES // rank
    pieces = rank // repeat
    step_width = width // chunks

    def load(source, target, sem):
        copy = pltpu.make_async_copy(source, target, sem)
        copy.start()
        return copy

    proj_out_copy = load(proj_out_hbm, proj_out, load_sem.at[0])
    grad_copy = load(grad_hbm, grad, load_sem.at[1])
    hidden_copies = []
    for c in range(chunks):
        part = pl.ds(c * step_width, step_width)
        hidden_copies.append(
            (
                load(proj_in_hbm.at[:, part], proj_in.at[:, part], hidden_sem.at[0, c]),
                load(hidden_hbm.at[:, :, part], hidden.at[:, :, part], hidden_sem.at[1, c]),
            )
        )
    own_query = my_dp if gathered else 0
    query_copy = load(query_hbm, query.at[own_query], load_sem.at[2])
    lengths_copy = load(lengths_hbm, lengths_ref, load_sem.at[3])

    barrier = pltpu.get_barrier_semaphore()

    def place(step):
        slot = lax.rem(me + step, planes)
        return slot, {"dp": lax.rem(slot, dp_size), "query": slot // dp_size}

    def greet(step):
        pl.semaphore_signal(barrier, inc=1, device_id=place(step)[1], device_id_type=MESH)

    pl.semaphore_signal(barrier, inc=1, device_id={"mp": other}, device_id_type=MESH)
    each(planes, greet)

    pl.semaphore_wait(barrier, planes)

    def exchange(which):
        copy = pltpu.make_async_remote_copy(
            src_ref=sums.at[which],
            dst_ref=pair.at[which],
            send_sem=pair_send.at[which],
            recv_sem=pair_recv.at[which],
            device_id={"mp": other},
            device_id_type=MESH,
        )
        copy.start()
        return copy

    beside = my_dp + 1 - 2 * lax.rem(my_dp, 2)
    across = lax.rem(my_dp + 2, 4)
    middle = (my_dp == 1) | (my_dp == 2)

    def query_to(which, half, slot, target, source=None):
        return pltpu.make_async_remote_copy(
            src_ref=query_hbm.at[my_mp, half] if source is None else source,
            dst_ref=query.at[slot, my_mp, half],
            send_sem=query_send.at[which, half],
            recv_sem=query_recv.at[which, half],
            device_id={"dp": target},
            device_id_type=MESH,
        )

    def query_share(slot, half):
        return pltpu.make_async_remote_copy(
            src_ref=query.at[slot, half],
            dst_ref=query.at[slot, half],
            send_sem=share_send.at[slot],
            recv_sem=share_recv.at[slot],
            device_id={"mp": other},
            device_id_type=MESH,
        )

    def dp_slot(step):
        return lax.rem(my_dp + step, dp_size)

    if gathered:
        query_to(0, 0, my_dp, 3 - my_dp).start()
        query_to(0, 1, my_dp, 3 - my_dp).start()

        @pl.when(jnp.logical_not(middle))
        def _():
            query_to(2, 0, my_dp, across).start()

        query_to(2, 1, my_dp, across).start()
        for half in range(2):
            query_to(1, half, my_dp, beside).start()

    proj_out_copy.wait()
    to_row = lax.broadcasted_iota(jnp.int32, (rank, rank), 0)
    from_row = lax.broadcasted_iota(jnp.int32, (rank, rank), 1)
    wanted = repeat * lax.rem(to_row, pieces) + to_row // pieces
    order = jnp.where(from_row == wanted, 1.0, 0.0).astype(jnp.bfloat16)
    ordered = jnp.dot(
        order, proj_out[...], preferred_element_type=jnp.float32
    ).astype(jnp.bfloat16)
    grad_copy.wait()
    for e in range(examples):
        sums[0, e] = dot_last(grad[e], ordered).T

    out_exchange = exchange(0)
    in_sums = [jnp.zeros((seq, rank), jnp.float32) for _ in range(examples)]
    for c in range(chunks):
        for copy in hidden_copies[c]:
            copy.wait()
        part = pl.ds(c * step_width, step_width)
        for e in range(examples):
            in_sums[e] += dot_last(hidden[e, :, part], proj_in[:, part])
    for e in range(examples):
        sums[1, e] = in_sums[e].T
    query_copy.wait()
    lengths_copy.wait()
    in_exchange = exchange(1)
    out_exchange.wait()
    positions = my_query * seq + lax.broadcasted_iota(jnp.int32, (1, seq), 1)
    weighted = []
    for e in range(examples):
        used = jnp.full((1, seq), lengths_ref[e], jnp.int32)
        weights = jnp.where(positions < used, 1.0 / jnp.sqrt(used.astype(jnp.float32)), 0.0)
        weighted.append((sums[0, e] + pair[0, e]) * weights)
    in_exchange.wait()
    lanes = lax.broadcasted_iota(jnp.int32, (pieces, LANES), 1) // rank
    for e in range(examples):
        inputs = sums[1, e] + pair[1, e]
        product = dot_last(
            weighted[e], jnp.concatenate([inputs] * repeat, axis=0), lax.Precision.HIGHEST
        )
        flat = product[:pieces]
        for r in range(1, repeat):
            flat = jnp.where(lanes == r, product[r * pieces : (r + 1) * pieces], flat)
        grads[me, e * pieces : (e + 1) * pieces] = flat

    def grads_copy(slot, target):
        return pltpu.make_async_remote_copy(
            src_ref=grads.at[slot],
            dst_ref=grads.at[slot],
            send_sem=grads_send.at[target],
            recv_sem=grads_recv.at[slot],
            device_id=target_id(target),
            device_id_type=MESH,
        )

    def target_id(slot):
        return {"dp": lax.rem(slot, dp_size), "query": slot // dp_size}

    def send_grads(step):
        grads_copy(me, place(step)[0]).start()

    def wait_grads(step):
        slot = place(step)[0]
        grads_copy(slot, slot).wait_recv()

    def wait_sent(step):
        grads_copy(me, place(step)[0]).wait_send()

    each(planes, send_grads)
    if gathered:
        query_to(0, 0, 3 - my_dp, 3 - my_dp).wait_recv()

        @pl.when(middle)
        def _():
            inner = 3 - my_dp
            query_to(2, 0, inner, beside, query.at[inner, my_mp, 0]).start()

        query_to(0, 1, 3 - my_dp, 3 - my_dp).wait_recv()
        query_share(3 - my_dp, my_mp).start()
        for half in range(2):
            query_to(1, half, beside, beside).wait_recv()
        query_share(beside, my_mp).start()
        for half in range(2):
            query_to(2, half, across, across).wait_recv()
        query_share(across, my_mp).start()
    each(planes, wait_grads)

    pieces_of = []
    flat_grads = grads.reshape(planes * examples * pieces, LANES)
    for p in range(pieces):
        piece = flat_grads[pl.ds(p, total, stride=pieces)]
        for q in range(1, query_size):
            piece += flat_grads[pl.ds(q * total * pieces + p, total, stride=pieces)]
        pieces_of.append(piece)
    vectors = jnp.concatenate(pieces_of, axis=1)
    blocks = LANES // queries
    shift = DAMPING * total
    solve = solve_few if total <= SUBLANES else solve_many
    if gathered:
        solved = solve(vectors, vectors * shift, shift)
        for step in range(1, dp_size):
            query_share(dp_slot(step), other).wait_recv()
        scores = dot_split(solved, query[...].reshape(dp_size * queries, features))
        mine = scores[:examples]
        for d in range(1, dp_size):
            mine = jnp.where(my_dp == d, scores[d * examples : (d + 1) * examples], mine)
        out_ref[...] = mine
        each(planes, wait_sent)
        for step in range(1, dp_size):
            for half in range(2):
                query_to(step - 1, half, my_dp, dp_slot(step)).wait_send()
            query_share(dp_slot(step), my_mp).wait_send()
        return
    rhs = dot_last(
        vectors, jnp.concatenate([query[0].reshape(queries, features)] * blocks, axis=0), lax.Precision.HIGHEST
    )
    solved = solve(vectors, rhs * shift, shift)
    block_of_lane = lax.broadcasted_iota(jnp.int32, (total, LANES), 1) // queries
    solved = jnp.where(block_of_lane == lax.rem(my_dp, blocks), solved, 0.0)
    for d in range(dp_size):
        sent[d, :examples] = solved[d * examples : (d + 1) * examples]

    def score_copy(slot, target):
        return pltpu.make_async_remote_copy(
            src_ref=sent.at[target],
            dst_ref=landed.at[slot],
            send_sem=score_send.at[target],
            recv_sem=score_recv.at[slot],
            device_id={"dp": target},
            device_id_type=MESH,
        )

    def send_score(step):
        score_copy(my_dp, lax.rem(my_dp + step, dp_size)).start()

    def wait_score(step):
        slot = lax.rem(my_dp + step, dp_size)
        score_copy(slot, slot).wait_recv()

    def wait_score_sent(step):
        score_copy(my_dp, lax.rem(my_dp + step, dp_size)).wait_send()

    each(dp_size, send_score)
    landed[my_dp] = sent[my_dp]
    each(planes, wait_sent)
    each(dp_size, wait_score)
    for b in range(dp_size // blocks):
        block = landed[b * blocks]
        for d in range(b * blocks + 1, (b + 1) * blocks):
            block += landed[d]
        out_ref[:, b * LANES : (b + 1) * LANES] = block[:examples]
    each(dp_size, wait_score_sent)


def shards(sizes, hidden_in, out_grad, proj_in, proj_out, lengths, query_grads):
    dp_size, query_size, mp_size = sizes
    examples, seq, _ = hidden_in.shape
    rank = proj_in.shape[0]
    queries, flat = query_grads.shape
    query_grads = query_grads.reshape(mp_size, 2, queries // mp_size // 2, flat)
    held = dp_size if dp_size == 4 else 1
    planes = dp_size * query_size
    pieces = flat // LANES
    chunks = 4
    hbm = pl.BlockSpec(memory_space=pl.ANY)
    dma = pltpu.SemaphoreType.DMA
    sums = pltpu.VMEM((2, examples, rank, seq), jnp.float32)
    scores = pltpu.VMEM((dp_size, SUBLANES, LANES), jnp.float32)
    return pl.pallas_call(
        functools.partial(kernel, sizes, chunks),
        out_shape=jax.ShapeDtypeStruct((examples, dp_size * queries), jnp.float32),
        in_specs=[hbm, hbm, hbm, hbm, hbm, hbm],
        out_specs=pl.BlockSpec(memory_space=pltpu.VMEM),
        scratch_shapes=[
            pltpu.VMEM(hidden_in.shape, hidden_in.dtype),
            pltpu.VMEM(out_grad.shape, out_grad.dtype),
            pltpu.VMEM(proj_in.shape, proj_in.dtype),
            pltpu.VMEM(proj_out.shape, proj_out.dtype),
            pltpu.SMEM(lengths.shape, lengths.dtype),
            pltpu.VMEM((held, *query_grads.shape), query_grads.dtype),
            sums,
            sums,
            pltpu.VMEM((planes, examples * pieces, LANES), jnp.float32),
            scores,
            scores,
            dma((4,)),
            dma((2, chunks)),
            dma((2,)),
            dma((2,)),
            dma((planes,)),
            dma((planes,)),
            dma((dp_size,)),
            dma((dp_size,)),
            dma((3, 2)),
            dma((3, 2)),
            dma((held,)),
            dma((held,)),
        ],
        compiler_params=pltpu.CompilerParams(
            collective_id=0, has_side_effects=True, vmem_limit_bytes=32 * 1024 * 1024
        ),
    )(*(pltpu.with_memory_space_constraint(a, pltpu.HBM) for a in (hidden_in, out_grad, proj_in, proj_out, lengths, query_grads)))


def solution(mesh):
    sizes = tuple(mesh.shape[a] for a in ("dp", "query", "mp"))
    in_specs = (
        P(("groups", "dp"), "query", "mp"),
        P(("groups", "dp"), "query", "mp"),
        P(None, "mp"),
        P(None, "mp"),
        P(("groups", "dp")),
        P(("groups", "query", "dp"), None),
    )
    out_specs = P(("groups", "dp"), "query")
    return jax.shard_map(
        functools.partial(shards, sizes),
        mesh=mesh,
        in_specs=in_specs,
        out_specs=out_specs,
        check_vma=False,
    )
```
